512 devices in a mesh: slab: 32 (over z_hi, x, core), trace: 16 (over y, z_lo).
Axes of the slice: x: 4, y: 4, z: 16 (z_hi: 4, z_lo: 4; z = z_hi * 4 + z_lo), core: 2. Of those that a mesh axis runs over, the one named last changes fastest.
Arguments:
- transmission: bfloat16 [32, 2048, 2048], P('slab', None, 'trace'), may hold values from -0.125 to 0.125
- reflection: bfloat16 [32, 2048, 2048], P('slab', None, 'trace'), may hold values from -0.0625 to 0.0625
- response: bfloat16 [32, 2048, 2048], P('slab', None, 'trace'), may hold values from -0.125 to 0.125
- sources: bfloat16 [32, 8, 32, 2048], P('slab', None, None, 'trace'), may hold values from -6 to 6
- placement: int32 [8, 32], replicated, may hold values from 0 to 31
Outputs:
- field_trace: bfloat16 [32, 8, 32, 2048], P('slab', None, None, 'trace')
The draws below stay inside these ranges and needn't reach their ends.
All inputs are finite; a program needn't handle non-finite values.
Results may differ from the reference program's by a relative error of at most 0.018.
Values may be sent and summed in bfloat16 or wider, within the bound.
A program may use at most 64 MiB of HBM per device.

```python
import jax
import jax.numpy as jnp
from jax import lax

TW = 2048
BATCH = 32
TICKS = 8
SLABS = 32


def touch_ends(result, rng, least, top_value):
    place = [jax.random.randint(jax.random.fold_in(rng, axis), (), 0, length) for axis, length in enumerate(result.shape)]
    widest = result.shape.index(max(result.shape))
    next_to = place[:widest] + [(place[widest] + 1) % result.shape[widest]] + place[widest + 1:]
    return result.at[tuple(place)].set(least).at[tuple(next_to)].set(top_value)


def shard_levels(key, shape, pieces, smallest, high):
    def one(axis_at, blocks):
        draws = jax.random.uniform(jax.random.fold_in(jax.random.fold_in(key, 6), axis_at), (blocks,), jnp.float32, smallest / len(pieces), high / len(pieces))
        return jnp.repeat(jnp.exp(draws), shape[axis_at] // blocks).reshape((-1,) + (1,) * (len(shape) - axis_at - 1))

    gain = one(*pieces[0])
    for cut in pieces[1:]:
        gain = gain * one(*cut)
    return gain


def scatter_about(own_key, shape, spread, limit, split=(), kind=jnp.bfloat16):
    array = spread * jax.random.normal(own_key, shape, jnp.float32)
    if split:
        array = array * shard_levels(own_key, shape, split, -0.22, 0.18)
    return jnp.clip(array, -limit, limit).astype(kind)


def setup_inputs(seed: int = 0) -> dict:
    key_of = jax.random.split(jax.random.key(seed), 6)
    transmission = scatter_about(key_of[0], (SLABS, TW, TW), (TW + TW // 9) ** -0.5, 0.125, ((0, 32), (2, 16)))
    reflection = scatter_about(key_of[1], (SLABS, TW, TW), (4 * TW) ** -0.5, 0.0625, ((0, 32), (2, 16)))
    response = scatter_about(key_of[2], (SLABS, TW, TW), TW ** -0.5, 0.125, ((0, 32), (2, 16)))
    sources = scatter_about(key_of[3], (SLABS, TICKS, BATCH, TW), 1.0, 6.0, ((0, 32), (3, 16)))
    placement = touch_ends(jax.random.randint(key_of[4], (TICKS, BATCH), 0, SLABS), jax.random.fold_in(key_of[4], 1), 0, SLABS - 1).astype(jnp.int32)
    return {"transmission": transmission, "reflection": reflection, "response": response, "sources": sources, "placement": placement}


def reference(transmission, reflection, response, sources, placement):
    slab_ids = jnp.arange(SLABS, dtype=jnp.int32)
    distance = jnp.abs(slab_ids[:, None, None] - placement[None, :, :]).astype(jnp.float32)
    weighting = 1.0 / (1.0 + distance)
    weighted = (sources.astype(jnp.float32) * weighting[..., None]).astype(jnp.bfloat16)
    flat = weighted.reshape(SLABS, TICKS * BATCH, TW)

    def respond(pair):
        return jnp.dot(pair[0], pair[1], preferred_element_type=jnp.float32)

    driven = lax.map(respond, (flat, response))

    def carry_along(incoming, pair):
        matrix, driven_here = pair
        fresh = (jnp.dot(incoming, matrix, preferred_element_type=jnp.float32) + driven_here).astype(jnp.bfloat16)
        return fresh, fresh

    initial = jnp.zeros((TICKS * BATCH, TW), jnp.bfloat16)
    ignored, down = lax.scan(carry_along, initial, (transmission, driven))
    ignored_up, up = lax.scan(carry_along, initial, (transmission, driven), reverse=True)
    contrast = (down.astype(jnp.float32) - up.astype(jnp.float32)).astype(jnp.bfloat16)

    def combine(quad):
        reflected = jnp.dot(quad[0], quad[3], preferred_element_type=jnp.float32)
        return (quad[1].astype(jnp.float32) + quad[2].astype(jnp.float32) + reflected).astype(jnp.bfloat16)

    field_trace = lax.map(combine, (contrast, down, up, reflection))
    return field_trace.reshape(SLABS, TICKS, BATCH, TW)
```

```python
import functools

import jax
import jax.numpy as jnp
from jax import lax
from jax.experimental import pallas as pl
from jax.experimental.pallas import tpu as pltpu
from jax.sharding import Mesh
from jax.sharding import PartitionSpec as P

TRACE = ("trace_0", "trace_1")
MESH = pl.DeviceIdType.MESH
CHUNKS = 4
FUSE_FROM = 4


def dot(a, b):
    return jnp.dot(a, b, preferred_element_type=jnp.float32)


def chain_kernel(
    slabs,
    t_ref,
    drv_ref,
    contrast_ref,
    total_ref,
    t_own,
    t_oth,
    fused,
    drv_oth,
    local,
    x_in,
    z_out,
    z_in,
    y_own,
    load_sem,
    t_send,
    t_recv,
    d_send,
    d_recv,
    x_send,
    x_recv,
    z_send,
    z_recv,
):
    slab = lax.axis_index("slab")
    row = lax.axis_index("trace_0")
    col = lax.axis_index("trace_1")
    core = slab % 2
    chip = slab // 2
    last = slabs // 2 - 1
    place = chip * (1 - 2 * core) + last * core
    partner = (slab + 1 - 2 * core, row, col)
    following = ((slab + 2 - 4 * core + slabs) % slabs, row, col)
    previous = ((slab - 2 + 4 * core + slabs) % slabs, row, col)
    width = t_own.shape[0]
    step = width // CHUNKS

    barrier = pltpu.get_barrier_semaphore()
    for device in (partner, following, previous):
        pl.semaphore_signal(barrier, inc=1, device_id=device, device_id_type=MESH)
    pl.semaphore_wait(barrier, 3)

    give_t = pltpu.make_async_remote_copy(
        src_ref=t_ref, dst_ref=t_oth, send_sem=t_send, recv_sem=t_recv, device_id=partner, device_id_type=MESH
    )
    give_t.start()
    give_d = pltpu.make_async_remote_copy(
        src_ref=drv_ref, dst_ref=drv_oth, send_sem=d_send, recv_sem=d_recv, device_id=partner, device_id_type=MESH
    )
    give_d.start()
    load = pltpu.make_async_copy(t_ref, t_own, load_sem)
    load.start()
    load.wait()
    give_d.wait()
    give_t.wait()

    def columns(j):
        return pl.ds(j * step, step)

    def onward(j):
        return pltpu.make_async_remote_copy(
            src_ref=z_out.at[:, columns(j)],
            dst_ref=x_in.at[:, columns(j)],
            send_sem=x_send.at[j],
            recv_sem=x_recv.at[j],
            device_id=following,
            device_id_type=MESH,
        )

    def emit(j, value):
        z_out[:, columns(j)] = value.astype(jnp.bfloat16)

        @pl.when(place < last)
        def _():
            onward(j).start()

    @pl.when(place == 0)
    def _():
        y_own[...] = drv_ref[...].astype(jnp.bfloat16)
        for j in range(CHUNKS):
            emit(j, dot(y_own[...], t_oth[:, columns(j)]) + drv_oth[:, columns(j)])

    @pl.when((place > 0) & (place < FUSE_FROM))
    def _():
        for j in range(CHUNKS):
            onward(j).wait_recv()
        for j in range(CHUNKS):
            here = dot(x_in[...], t_own[:, columns(j)]) + drv_ref[:, columns(j)]
            y_own[:, columns(j)] = here.astype(jnp.bfloat16)
        for j in range(CHUNKS):
            emit(j, dot(y_own[...], t_oth[:, columns(j)]) + drv_oth[:, columns(j)])

    @pl.when(place >= FUSE_FROM)
    def _():
        local[...] = dot(drv_ref[...].astype(jnp.bfloat16), t_oth[...]) + drv_oth[...]
        tall, wide = width // 4, width // 8

        def block(i, carry):
            rows = pl.ds(pl.multiple_of((i % 4) * tall, tall), tall)
            cols = pl.ds(pl.multiple_of((i // 4) * wide, wide), wide)
            fused[rows, cols] = dot(t_own[rows, :], t_oth[:, cols]).astype(jnp.bfloat16)
            return carry

        lax.fori_loop(0, 32, block, 0)
        for j in range(CHUNKS):
            onward(j).wait_recv()
        for j in range(CHUNKS):
            emit(j, dot(x_in[...], fused[:, columns(j)]) + local[:, columns(j)])
        for j in range(CHUNKS):
            here = dot(x_in[...], t_own[:, columns(j)]) + drv_ref[:, columns(j)]
            y_own[:, columns(j)] = here.astype(jnp.bfloat16)

    swap = pltpu.make_async_remote_copy(
        src_ref=z_out, dst_ref=z_in, send_sem=z_send, recv_sem=z_recv, device_id=partner, device_id_type=MESH
    )
    swap.start()
    swap.wait()
    mine = y_own[...].astype(jnp.float32)
    other = z_in[...].astype(jnp.float32)
    sign = (1 - 2 * core).astype(jnp.float32)
    contrast_ref[...] = ((mine - other) * sign).astype(jnp.bfloat16)
    total_ref[...] = (mine + other).astype(jnp.bfloat16)

    @pl.when(place < last)
    def _():
        for j in range(CHUNKS):
            onward(j).wait_send()


def run_chain(transfer, driven, slabs):
    rows, width = driven.shape
    vmem = pl.BlockSpec(memory_space=pltpu.VMEM)
    dma = pltpu.SemaphoreType.DMA
    trace = jax.ShapeDtypeStruct((rows, width), jnp.bfloat16)
    operator = pltpu.VMEM((width, width), jnp.bfloat16)
    narrow = pltpu.VMEM((rows, width), jnp.bfloat16)
    full = pltpu.VMEM((rows, width), jnp.float32)
    return pl.pallas_call(
        functools.partial(chain_kernel, slabs),
        out_shape=(trace, trace),
        in_specs=[pl.BlockSpec(memory_space=pl.ANY), vmem],
        out_specs=(vmem, vmem),
        scratch_shapes=[operator, operator, operator, full, full, narrow, narrow, narrow, narrow]
        + [dma] * 5
        + [dma((CHUNKS,))] * 2
        + [dma] * 2,
        compiler_params=pltpu.CompilerParams(
            collective_id=0, has_side_effects=True, vmem_limit_bytes=48 * 2**20
        ),
        name="chain",
    )(transfer, driven)


def shards(slabs, transmission, reflection, response, sources, placement):
    transfer = transmission[0]
    reflect = reflection[0]
    respond = response[0]
    own_sources = sources[0]
    ticks, batch, depth = own_sources.shape
    rows = ticks * batch
    slab = lax.axis_index("slab")
    distance = jnp.abs(slab - placement).astype(jnp.float32)
    weighting = 1.0 / (1.0 + distance)
    weighted = (own_sources.astype(jnp.float32) * weighting[:, :, None]).astype(jnp.bfloat16)
    flat = weighted.reshape(rows, depth)
    every = lax.all_gather(flat, TRACE, axis=1, tiled=True)
    driven = dot(every, respond)
    nearer = lax.all_gather(transfer, "trace_1", axis=1, tiled=True)
    whole = lax.all_gather(nearer, "trace_0", axis=1, tiled=True)
    own_driven = lax.all_to_all(driven, TRACE, split_axis=0, concat_axis=1, tiled=True)
    contrast, total = run_chain(whole, own_driven, slabs)
    contrast = lax.all_gather(contrast, TRACE, axis=0, tiled=True)
    total = lax.all_to_all(total, TRACE, split_axis=1, concat_axis=0, tiled=True)
    combined = total.astype(jnp.float32) + dot(contrast, reflect)
    return combined.astype(jnp.bfloat16).reshape(1, ticks, batch, depth)


def solution(mesh):
    slabs = mesh.shape["slab"]
    torus = Mesh(mesh.devices.reshape(slabs, 4, 4), ("slab",) + TRACE)
    return jax.shard_map(
        functools.partial(shards, slabs),
        mesh=torus,
        in_specs=(
            P("slab", None, TRACE),
            P("slab", None, TRACE),
            P("slab", None, TRACE),
            P("slab", None, None, TRACE),
            P(),
        ),
        out_specs=P("slab", None, None, TRACE),
        check_vma=False,
    )
```

```python
import functools

import jax
import jax.numpy as jnp
from jax import lax
from jax.experimental import pallas as pl
from jax.experimental.pallas import tpu as pltpu
from jax.sharding import Mesh
from jax.sharding import PartitionSpec as P

TRACE = ("trace_0", "trace_1")
MESH = pl.DeviceIdType.MESH
SIDE = 4
CHUNKS = 4
FUSE_FROM = 6
bf16 = jnp.bfloat16
f32 = jnp.float32


def dot(a, b):
    return jnp.dot(a, b, preferred_element_type=f32)


def loop(count, body):
    def step(i, carry):
        body(i)
        return carry

    lax.fori_loop(0, count, step, 0)


class Spread:
    def __init__(self, place, own, view, sems, extra=None):
        self.slab, self.row, self.col = place
        self.own, self.view, self.extra = own, view, extra
        self.arrived, self.up, self.down, self.fore, self.back = sems

    def copies(self, source, block, half, up, down, fore, back, run):
        row, col = self.row, self.col

        def send(sem, device):
            run(
                pltpu.make_async_remote_copy(
                    src_ref=source,
                    dst_ref=self.view(block, half),
                    send_sem=sem.at[block, half],
                    recv_sem=self.arrived.at[block, half],
                    device_id=device,
                    device_id_type=MESH,
                )
            )

        @pl.when(up)
        def _():
            send(self.up, (self.slab, row, jnp.minimum(col + 1, SIDE - 1)))

        @pl.when(down)
        def _():
            send(self.down, (self.slab, row, jnp.maximum(col - 1, 0)))

        @pl.when(fore)
        def _():
            send(self.fore, (self.slab, (row + 1) % SIDE, col))

        @pl.when(back)
        def _():
            send(self.back, (self.slab, (row + SIDE - 1) % SIDE, col))

        if self.extra is not None:
            run(self.extra(source, block, half))

    def await_piece(self, block, half):
        piece = self.view(block, half)
        pltpu.make_async_copy(piece, piece, self.arrived.at[block, half]).wait()

    def first(self, run):
        yes = self.row >= 0
        block = self.row * SIDE + self.col

        def piece(half):
            self.copies(self.own(half), block, half, self.col < SIDE - 1, self.col > 0, yes, yes, run)

        loop(2, piece)

    def rest(self, run, receive):
        row, col = self.row, self.col
        yes, no = row >= 0, row < 0

        def pieces(distance, body):
            def one(i):
                side = 2 * (i // 2) - 1
                at = col + side * distance
                there = (at >= 0) & (at < SIDE) & (distance >= 0) & ((distance > 0) | (side < 0))

                @pl.when(there)
                def _():
                    body(side, at, i % 2)

            loop(4, one)

        def handle(block, half, up, down, fore, back):
            if receive:
                self.await_piece(block, half)
            self.copies(self.view(block, half), block, half, up, down, fore, back, run)

        def along(side, at, half):
            up = (side < 0) & (col < SIDE - 1)
            down = (side > 0) & (col > 0)
            handle(row * SIDE + at, half, up, down, yes, yes)

        def around(side, at, half):
            handle((row + SIDE - 1) % SIDE * SIDE + at, half, no, no, half == 0, no)
            handle((row + 1) % SIDE * SIDE + at, half, no, no, no, half == 1)

        def across(side, at, half):
            handle((row + 2) % SIDE * SIDE + at, half, no, no, no, no)

        def turn(r):
            @pl.when(r < SIDE - 1)
            def _():
                pieces(r + 1, along)

            pieces(r, around)
            pieces(r - 1, across)

        loop(SIDE + 1, turn)


def start(copy):
    copy.start()


def wait_send(copy):
    copy.wait_send()


def sweep_kernel(
    slabs,
    transfer_ref,
    respond_ref,
    reflect_ref,
    weighted_ref,
    out_ref,
    t_own,
    t_oth,
    fused,
    respond,
    reflect,
    sources,
    driven,
    drv_own,
    drv_oth,
    local,
    x_in,
    z_out,
    z_in,
    y_own,
    contrast,
    total,
    totals,
    load_sem,
    d_send,
    d_recv,
    x_send,
    x_recv,
    z_send,
    z_recv,
    exchange_send,
    exchange_recv,
    core_send,
    core_recv,
    *spread_sems,
):
    slab = lax.axis_index("slab")
    row = lax.axis_index("trace_0")
    col = lax.axis_index("trace_1")
    trace = row * SIDE + col
    peers = SIDE * SIDE
    core = slab % 2
    chip = slab // 2
    last = slabs // 2 - 1
    place = chip * (1 - 2 * core) + last * core
    partner = (slab + 1 - 2 * core, row, col)
    following = ((slab + 2 - 4 * core + slabs) % slabs, row, col)
    previous = ((slab - 2 + 4 * core + slabs) % slabs, row, col)
    width = t_own.shape[0]
    depth = respond.shape[1]
    rows = sources.shape[0]
    share = rows // peers
    step = width // CHUNKS

    def peer(j):
        other = (trace + 1 + j) % peers
        return other, (slab, other // SIDE, other % SIDE)

    barrier = pltpu.get_barrier_semaphore()

    def greet(j):
        pl.semaphore_signal(barrier, inc=1, device_id=peer(j)[1], device_id_type=MESH)

    for device in (partner, following, previous):
        pl.semaphore_signal(barrier, inc=1, device_id=device, device_id_type=MESH)
    loop(peers - 1, greet)

    def block_columns(b):
        return pl.ds(pl.multiple_of(b * depth, depth), depth)

    def block_rows(b):
        return pl.ds(pl.multiple_of(b * share, share), share)

    loads = [
        pltpu.make_async_copy(transfer_ref, t_own.at[:, block_columns(trace)], load_sem.at[0]),
        pltpu.make_async_copy(weighted_ref, sources.at[:, block_columns(trace)], load_sem.at[1]),
        pltpu.make_async_copy(respond_ref, respond, load_sem.at[2]),
        pltpu.make_async_copy(reflect_ref, reflect, load_sem.at[3]),
    ]
    for load in loads:
        load.start()
    pl.semaphore_wait(barrier, peers + 2)

    def half_rows(count, half):
        return pl.ds(pl.multiple_of(half * (count // 2), count // 2), count // 2)

    here = (slab, row, col)

    def to_partner(source, block, half):
        return pltpu.make_async_remote_copy(
            src_ref=source,
            dst_ref=t_oth.at[half_rows(width, half), block_columns(block)],
            send_sem=core_send.at[block, half],
            recv_sem=core_recv.at[block, half],
            device_id=partner,
            device_id_type=MESH,
        )

    source_spread = Spread(
        here,
        lambda half: weighted_ref.at[half_rows(rows, half), :],
        lambda block, half: sources.at[half_rows(rows, half), block_columns(block)],
        spread_sems[0:5],
    )
    transfer_spread = Spread(
        here,
        lambda half: transfer_ref.at[half_rows(width, half), :],
        lambda block, half: t_own.at[half_rows(width, half), block_columns(block)],
        spread_sems[5:10],
        to_partner,
    )
    contrast_spread = Spread(
        here,
        lambda half: contrast.at[block_rows(trace), half_rows(width, half)],
        lambda block, half: contrast.at[block_rows(block), half_rows(width, half)],
        spread_sems[10:15],
    )

    source_spread.first(start)
    transfer_spread.first(start)
    source_spread.rest(start, True)
    for load in loads:
        load.wait()

    driven[...] = dot(sources[...], respond[...])

    def give_driven(j):
        other, device = peer(j)
        return pltpu.make_async_remote_copy(
            src_ref=driven.at[block_rows(other), :],
            dst_ref=drv_own.at[:, block_columns(trace)],
            send_sem=exchange_send.at[0, other],
            recv_sem=exchange_recv.at[0, trace],
            device_id=device,
            device_id_type=MESH,
        )

    loop(peers - 1, lambda j: give_driven(j).start())
    drv_own[:, block_columns(trace)] = driven[block_rows(trace), :]

    transfer_spread.rest(start, True)

    def take_driven(j):
        other, _ = peer(j)
        piece = drv_own.at[:, block_columns(other)]
        pltpu.make_async_copy(piece, piece, exchange_recv.at[0, other]).wait()

    loop(peers - 1, take_driven)
    give_d = pltpu.make_async_remote_copy(
        src_ref=drv_own, dst_ref=drv_oth, send_sem=d_send, recv_sem=d_recv, device_id=partner, device_id_type=MESH
    )
    give_d.start()

    def take_transfer(i):
        piece = t_oth.at[half_rows(width, i % 2), block_columns(i // 2)]
        pltpu.make_async_copy(piece, piece, core_recv.at[i // 2, i % 2]).wait()

    loop(2 * peers, take_transfer)
    give_d.wait()

    def columns(j):
        return pl.ds(j * step, step)

    def onward(j):
        return pltpu.make_async_remote_copy(
            src_ref=z_out.at[:, columns(j)],
            dst_ref=x_in.at[:, columns(j)],
            send_sem=x_send.at[j],
            recv_sem=x_recv.at[j],
            device_id=following,
            device_id_type=MESH,
        )

    def emit(j, value):
        z_out[:, columns(j)] = value.astype(bf16)

        @pl.when(place < last)
        def _():
            onward(j).start()

    @pl.when(place == 0)
    def _():
        y_own[...] = drv_own[...].astype(bf16)
        for j in range(CHUNKS):
            emit(j, dot(y_own[...], t_oth[:, columns(j)]) + drv_oth[:, columns(j)])

    @pl.when((place > 0) & (place < FUSE_FROM))
    def _():
        for j in range(CHUNKS):
            onward(j).wait_recv()
        for j in range(CHUNKS):
            value = dot(x_in[...], t_own[:, columns(j)]) + drv_own[:, columns(j)]
            y_own[:, columns(j)] = value.astype(bf16)
        for j in range(CHUNKS):
            emit(j, dot(y_own[...], t_oth[:, columns(j)]) + drv_oth[:, columns(j)])

    @pl.when(place >= FUSE_FROM)
    def _():
        local[...] = dot(drv_own[...].astype(bf16), t_oth[...]) + drv_oth[...]
        tall, wide = width // 4, width // 8

        def block(i):
            at = pl.ds(pl.multiple_of((i % 4) * tall, tall), tall)
            to = pl.ds(pl.multiple_of((i // 4) * wide, wide), wide)
            fused[at, to] = dot(t_own[at, :], t_oth[:, to]).astype(bf16)

        loop(32, block)
        for j in range(CHUNKS):
            onward(j).wait_recv()
        for j in range(CHUNKS):
            emit(j, dot(x_in[...], fused[:, columns(j)]) + local[:, columns(j)])
        for j in range(CHUNKS):
            value = dot(x_in[...], t_own[:, columns(j)]) + drv_own[:, columns(j)]
            y_own[:, columns(j)] = value.astype(bf16)

    swap = pltpu.make_async_remote_copy(
        src_ref=z_out, dst_ref=z_in, send_sem=z_send, recv_sem=z_recv, device_id=partner, device_id_type=MESH
    )
    swap.start()
    swap.wait()
    mine = y_own[...].astype(f32)
    other_way = z_in[...].astype(f32)
    sign = (1 - 2 * core).astype(f32)
    contrast[block_rows(trace), :] = ((mine - other_way) * sign).astype(bf16)
    total[...] = mine + other_way
    contrast_spread.first(start)

    def give_total(j):
        other, device = peer(j)
        return pltpu.make_async_remote_copy(
            src_ref=total.at[:, block_columns(other)],
            dst_ref=totals.at[block_rows(trace), :],
            send_sem=exchange_send.at[1, other],
            recv_sem=exchange_recv.at[1, trace],
            device_id=device,
            device_id_type=MESH,
        )

    loop(peers - 1, lambda j: give_total(j).start())
    totals[block_rows(trace), :] = total[:, block_columns(trace)]
    contrast_spread.rest(start, True)

    def take_total(j):
        other, _ = peer(j)
        piece = totals.at[block_rows(other), :]
        pltpu.make_async_copy(piece, piece, exchange_recv.at[1, other]).wait()

    loop(peers - 1, take_total)
    out_ref[...] = (totals[...] + dot(contrast[...], reflect[...])).astype(bf16)

    @pl.when(place < last)
    def _():
        for j in range(CHUNKS):
            onward(j).wait_send()

    loop(peers - 1, lambda j: give_driven(j).wait_send())
    loop(peers - 1, lambda j: give_total(j).wait_send())
    for spread in (source_spread, transfer_spread, contrast_spread):
        spread.first(wait_send)
        spread.rest(wait_send, False)


def sweep(transfer, respond, reflect, weighted, slabs):
    width, depth = transfer.shape
    rows = weighted.shape[0]
    peers = SIDE * SIDE
    share = rows // peers
    anywhere = pl.BlockSpec(memory_space=pl.ANY)
    vmem = pl.BlockSpec(memory_space=pltpu.VMEM)
    dma = pltpu.SemaphoreType.DMA
    operator = pltpu.VMEM((width, width), bf16)
    narrow = pltpu.VMEM((share, width), bf16)
    full = pltpu.VMEM((share, width), f32)
    return pl.pallas_call(
        functools.partial(sweep_kernel, slabs),
        out_shape=jax.ShapeDtypeStruct((rows, depth), bf16),
        in_specs=[anywhere] * 4,
        out_specs=vmem,
        scratch_shapes=[
            operator,
            operator,
            operator,
            pltpu.VMEM((width, depth), bf16),
            pltpu.VMEM((width, depth), bf16),
            pltpu.VMEM((rows, width), bf16),
            pltpu.VMEM((rows, depth), f32),
            full,
            full,
            full,
            narrow,
            narrow,
            narrow,
            narrow,
            pltpu.VMEM((rows, width), bf16),
            full,
            pltpu.VMEM((rows, depth), f32),
            dma((4,)),
            dma,
            dma,
            dma((CHUNKS,)),
            dma((CHUNKS,)),
            dma,
            dma,
            dma((2, peers)),
            dma((2, peers)),
            dma((peers, 2)),
            dma((peers, 2)),
        ]
        + [dma((peers, 2))] * 15,
        compiler_params=pltpu.CompilerParams(
            collective_id=0, has_side_effects=True, vmem_limit_bytes=44 * 2**20
        ),
        name="sweep",
    )(transfer, respond, reflect, weighted)


def shards(slabs, transmission, reflection, response, sources, placement):
    own_sources = sources[0]
    ticks, batch, depth = own_sources.shape
    rows = ticks * batch
    slab = lax.axis_index("slab")
    distance = jnp.abs(slab - placement).astype(f32)
    weighting = 1.0 / (1.0 + distance)
    weighted = (own_sources.astype(f32) * weighting[:, :, None]).astype(bf16)
    combined = sweep(
        transmission[0], response[0], reflection[0], weighted.reshape(rows, depth), slabs
    )
    return combined.reshape(1, ticks, batch, depth)


def solution(mesh):
    slabs = mesh.shape["slab"]
    torus = Mesh(mesh.devices.reshape(slabs, SIDE, SIDE), ("slab",) + TRACE)
    return jax.shard_map(
        functools.partial(shards, slabs),
        mesh=torus,
        in_specs=(
            P("slab", None, TRACE),
            P("slab", None, TRACE),
            P("slab", None, TRACE),
            P("slab", None, None, TRACE),
            P(),
        ),
        out_specs=P("slab", None, None, TRACE),
        check_vma=False,
    )
```

```python
import functools

import jax
import jax.numpy as jnp
from jax import lax
from jax.experimental import pallas as pl
from jax.experimental.pallas import tpu as pltpu
from jax.sharding import Mesh
from jax.sharding import PartitionSpec as P

TRACE = ("trace_0", "trace_1")
MESH = pl.DeviceIdType.MESH
SIDE = 4
CHUNKS = 4
FUSE_FROM = 4
RING_SHARE = 7 / 32
LAG = 2
bf16 = jnp.bfloat16
f32 = jnp.float32


def dot(a, b):
    return jnp.dot(a, b, preferred_element_type=f32)


def loop(count, body):
    def step(i, carry):
        body(i)
        return carry

    lax.fori_loop(0, count, step, 0)


class Spread:
    def __init__(self, place, own, view, sems, extra=None):
        self.slab, self.row, self.col = place
        self.own, self.view, self.extra = own, view, extra
        self.arrived, self.up, self.down, self.fore, self.back = sems

    def copies(self, source, block, half, up, down, fore, back, run):
        row, col = self.row, self.col

        def send(sem, device):
            run(
                pltpu.make_async_remote_copy(
                    src_ref=source,
                    dst_ref=self.view(block, half),
                    send_sem=sem.at[block, half],
                    recv_sem=self.arrived.at[block, half],
                    device_id=device,
                    device_id_type=MESH,
                )
            )

        @pl.when(up)
        def _():
            send(self.up, (self.slab, row, jnp.minimum(col + 1, SIDE - 1)))

        @pl.when(down)
        def _():
            send(self.down, (self.slab, row, jnp.maximum(col - 1, 0)))

        @pl.when(fore)
        def _():
            send(self.fore, (self.slab, (row + 1) % SIDE, col))

        @pl.when(back)
        def _():
            send(self.back, (self.slab, (row + SIDE - 1) % SIDE, col))

        if self.extra is not None:
            run(self.extra(source, block, half))

    def await_piece(self, block, half):
        piece = self.view(block, half)
        pltpu.make_async_copy(piece, piece, self.arrived.at[block, half]).wait()

    def first(self, run):
        yes = self.row >= 0
        block = self.row * SIDE + self.col

        def piece(half):
            self.copies(self.own(half), block, half, self.col < SIDE - 1, self.col > 0, yes, yes, run)

        loop(2, piece)

    def handle(self, block, half, up, down, fore, back, run, receive):
        if receive:
            self.await_piece(block, half)
        self.copies(self.view(block, half), block, half, up, down, fore, back, run)

    def pieces(self, distance, body):
        def one(i):
            side = 2 * (i // 2) - 1
            at = self.col + side * distance
            there = (at >= 0) & (at < SIDE) & (distance >= 0) & ((distance > 0) | (side < 0))

            @pl.when(there)
            def _():
                body(side, at, i % 2)

        loop(4, one)

    def turn(self, r, run, receive):
        row, col = self.row, self.col
        yes, no = row >= 0, row < 0

        def along(side, at, half):
            up = (side < 0) & (col < SIDE - 1)
            down = (side > 0) & (col > 0)
            self.handle(row * SIDE + at, half, up, down, yes, yes, run, receive)

        def around(side, at, half):
            self.handle((row + SIDE - 1) % SIDE * SIDE + at, half, no, no, half == 0, no, run, receive)
            self.handle((row + 1) % SIDE * SIDE + at, half, no, no, no, half == 1, run, receive)

        def across(side, at, half):
            self.handle((row + 2) % SIDE * SIDE + at, half, no, no, no, no, run, receive)

        @pl.when(r < SIDE - 1)
        def _():
            self.pieces(r + 1, along)

        self.pieces(r, around)
        self.pieces(r - 1, across)

    def rest(self, run, receive):
        loop(SIDE + 1, lambda r: self.turn(r, run, receive))


class RingFirst(Spread):
    def turn(self, r, run, receive):
        row, col = self.row, self.col
        no = row < 0
        rising, falling = col < SIDE - 1, col > 0

        @pl.when(r == 0)
        def _():
            def around(half):
                before = (row + SIDE - 1) % SIDE * SIDE + col
                after = (row + 1) % SIDE * SIDE + col
                self.handle(before, half, rising, falling, half == 0, no, run, receive)
                self.handle(after, half, rising, falling, no, half == 1, run, receive)

            loop(2, around)

        @pl.when(r == 1)
        def _():
            def across(half):
                self.handle((row + 2) % SIDE * SIDE + col, half, rising, falling, no, no, run, receive)

            loop(2, across)

        @pl.when(r > 1)
        def _():
            def along(j):
                block_row = (row + j + j // 2 * (5 - 2 * j)) % SIDE

                def piece(side, at, half):
                    up = (side < 0) & rising
                    down = (side > 0) & falling
                    self.handle(block_row * SIDE + at, half, up, down, no, no, run, receive)

                self.pieces(r - 1, piece)

            loop(SIDE, along)


def start(copy):
    copy.start()


def wait_send(copy):
    copy.wait_send()


def sweep_kernel(
    slabs,
    transfer_ref,
    respond_ref,
    reflect_ref,
    weighted_ref,
    out_ref,
    t_own,
    t_oth,
    fused,
    respond,
    reflect,
    sources,
    driven,
    drv_own,
    drv_oth,
    local,
    x_in,
    z_out,
    z_in,
    y_own,
    contrast,
    total,
    totals,
    load_sem,
    d_send,
    d_recv,
    x_send,
    x_recv,
    z_send,
    z_recv,
    exchange_send,
    exchange_recv,
    core_send,
    core_recv,
    *spread_sems,
):
    slab = lax.axis_index("slab")
    row = lax.axis_index("trace_0")
    col = lax.axis_index("trace_1")
    trace = row * SIDE + col
    peers = SIDE * SIDE
    core = slab % 2
    chip = slab // 2
    last = slabs // 2 - 1
    place = chip * (1 - 2 * core) + last * core
    partner = (slab + 1 - 2 * core, row, col)
    following = ((slab + 2 - 4 * core + slabs) % slabs, row, col)
    previous = ((slab - 2 + 4 * core + slabs) % slabs, row, col)
    width = t_own.shape[0]
    depth = respond.shape[1]
    rows = sources.shape[0]
    share = rows // peers
    step = width // CHUNKS

    def peer(j):
        other = (trace + 1 + j) % peers
        return other, (slab, other // SIDE, other % SIDE)

    barrier = pltpu.get_barrier_semaphore()

    def greet(j):
        pl.semaphore_signal(barrier, inc=1, device_id=peer(j)[1], device_id_type=MESH)

    for device in (partner, following, previous):
        pl.semaphore_signal(barrier, inc=1, device_id=device, device_id_type=MESH)
    loop(peers - 1, greet)

    def block_columns(b):
        return pl.ds(pl.multiple_of(b * depth, depth), depth)

    def block_rows(b):
        return pl.ds(pl.multiple_of(b * share, share), share)

    loads = [
        pltpu.make_async_copy(transfer_ref, t_own.at[:, block_columns(trace)], load_sem.at[0]),
        pltpu.make_async_copy(weighted_ref, sources.at[:, block_columns(trace)], load_sem.at[1]),
        pltpu.make_async_copy(respond_ref, respond, load_sem.at[2]),
        pltpu.make_async_copy(reflect_ref, reflect, load_sem.at[3]),
    ]
    for load in loads:
        load.start()
    pl.semaphore_wait(barrier, peers + 2)

    def half_rows(count, half):
        return pl.ds(pl.multiple_of(half * (count // 2), count // 2), count // 2)

    here = (slab, row, col)

    ring = int(width * RING_SHARE) // 32 * 32

    def part(which, half):
        lowest, size = ((0, ring // 2), (ring, (width - ring) // 2))[which]
        return pl.ds(pl.multiple_of(lowest + half * size, 16), size)

    def to_partner(which, source, block, half):
        return pltpu.make_async_remote_copy(
            src_ref=source,
            dst_ref=t_oth.at[part(which, half), block_columns(block)],
            send_sem=core_send.at[which, block, half],
            recv_sem=core_recv.at[which, block, half],
            device_id=partner,
            device_id_type=MESH,
        )

    def transfer_part(kind, which, sems):
        return kind(
            here,
            lambda half: transfer_ref.at[part(which, half), :],
            lambda block, half: t_own.at[part(which, half), block_columns(block)],
            sems,
            functools.partial(to_partner, which),
        )

    source_spread = Spread(
        here,
        lambda half: weighted_ref.at[half_rows(rows, half), :],
        lambda block, half: sources.at[half_rows(rows, half), block_columns(block)],
        spread_sems[0:5],
    )
    line_first = transfer_part(Spread, 1, spread_sems[5:10])
    ring_first = transfer_part(RingFirst, 0, spread_sems[15:20])
    contrast_spread = Spread(
        here,
        lambda half: contrast.at[block_rows(trace), half_rows(width, half)],
        lambda block, half: contrast.at[block_rows(block), half_rows(width, half)],
        spread_sems[10:15],
    )

    def give_driven(j):
        other, device = peer(j)
        return pltpu.make_async_remote_copy(
            src_ref=driven.at[block_rows(other), :],
            dst_ref=drv_own.at[:, block_columns(trace)],
            send_sem=exchange_send.at[0, other],
            recv_sem=exchange_recv.at[0, trace],
            device_id=device,
            device_id_type=MESH,
        )

    def take_driven(j):
        other, _ = peer(j)
        piece = drv_own.at[:, block_columns(other)]
        pltpu.make_async_copy(piece, piece, exchange_recv.at[0, other]).wait()

    give_d = pltpu.make_async_remote_copy(
        src_ref=drv_own, dst_ref=drv_oth, send_sem=d_send, recv_sem=d_recv, device_id=partner, device_id_type=MESH
    )

    source_spread.first(start)
    line_first.first(start)
    ring_first.first(start)
    turns = SIDE + 1
    for load in loads:
        load.wait()

    def gather(i):
        @pl.when(i < turns)
        def _():
            source_spread.turn(i, start, True)

        @pl.when(i == turns)
        def _():
            driven[...] = dot(sources[...], respond[...])
            loop(peers - 1, lambda j: give_driven(j).start())
            drv_own[:, block_columns(trace)] = driven[block_rows(trace), :]

        @pl.when(i == turns + LAG - 1)
        def _():
            loop(peers - 1, take_driven)
            give_d.start()

        @pl.when(i >= LAG)
        def _():
            line_first.turn(i - LAG, start, True)
            ring_first.turn(i - LAG, start, True)

    loop(turns + LAG, gather)

    def take_transfer(i):
        block, half = i // 2, i % 2
        for which in range(2):
            piece = t_oth.at[part(which, half), block_columns(block)]
            pltpu.make_async_copy(piece, piece, core_recv.at[which, block, half]).wait()

    loop(2 * peers, take_transfer)
    give_d.wait()

    def columns(j):
        return pl.ds(j * step, step)

    def onward(j):
        return pltpu.make_async_remote_copy(
            src_ref=z_out.at[:, columns(j)],
            dst_ref=x_in.at[:, columns(j)],
            send_sem=x_send.at[j],
            recv_sem=x_recv.at[j],
            device_id=following,
            device_id_type=MESH,
        )

    def emit(j, value):
        z_out[:, columns(j)] = value.astype(bf16)

        @pl.when(place < last)
        def _():
            onward(j).start()

    @pl.when(place == 0)
    def _():
        y_own[...] = drv_own[...].astype(bf16)
        for j in range(CHUNKS):
            emit(j, dot(y_own[...], t_oth[:, columns(j)]) + drv_oth[:, columns(j)])

    def take_rows(operator, store):
        final = CHUNKS - 1
        for j in range(final):
            onward(j).wait_recv()
            local[...] += dot(x_in[:, columns(j)], operator[columns(j), :])
        onward(final).wait_recv()
        for j in range(CHUNKS):
            store(j, local[:, columns(j)] + dot(x_in[:, columns(final)], operator[columns(final), columns(j)]))

    def keep(j, value):
        y_own[:, columns(j)] = value.astype(bf16)

    @pl.when((place > 0) & (place < FUSE_FROM))
    def _():
        local[...] = drv_own[...]
        take_rows(t_own, keep)
        for j in range(CHUNKS):
            emit(j, dot(y_own[...], t_oth[:, columns(j)]) + drv_oth[:, columns(j)])

    @pl.when(place >= FUSE_FROM)
    def _():
        local[...] = dot(drv_own[...].astype(bf16), t_oth[...]) + drv_oth[...]
        wide = width // 8

        def block(i):
            to = pl.ds(pl.multiple_of(i * wide, wide), wide)
            fused[:, to] = dot(t_own[...], t_oth[:, to]).astype(bf16)

        loop(8, block)
        take_rows(fused, emit)
        for j in range(CHUNKS):
            keep(j, dot(x_in[...], t_own[:, columns(j)]) + drv_own[:, columns(j)])

    swap = pltpu.make_async_remote_copy(
        src_ref=z_out, dst_ref=z_in, send_sem=z_send, recv_sem=z_recv, device_id=partner, device_id_type=MESH
    )
    swap.start()
    swap.wait()
    mine = y_own[...].astype(f32)
    other_way = z_in[...].astype(f32)
    sign = (1 - 2 * core).astype(f32)
    contrast[block_rows(trace), :] = ((mine - other_way) * sign).astype(bf16)
    total[...] = mine + other_way
    contrast_spread.first(start)

    def give_total(j):
        other, device = peer(j)
        return pltpu.make_async_remote_copy(
            src_ref=total.at[:, block_columns(other)],
            dst_ref=totals.at[block_rows(trace), :],
            send_sem=exchange_send.at[1, other],
            recv_sem=exchange_recv.at[1, trace],
            device_id=device,
            device_id_type=MESH,
        )

    loop(peers - 1, lambda j: give_total(j).start())
    totals[block_rows(trace), :] = total[:, block_columns(trace)]
    contrast_spread.rest(start, True)

    def take_total(j):
        other, _ = peer(j)
        piece = totals.at[block_rows(other), :]
        pltpu.make_async_copy(piece, piece, exchange_recv.at[1, other]).wait()

    loop(peers - 1, take_total)
    out_ref[...] = (totals[...] + dot(contrast[...], reflect[...])).astype(bf16)

    @pl.when(place < last)
    def _():
        for j in range(CHUNKS):
            onward(j).wait_send()

    loop(peers - 1, lambda j: give_driven(j).wait_send())
    loop(peers - 1, lambda j: give_total(j).wait_send())
    for spread in (source_spread, line_first, ring_first, contrast_spread):
        spread.first(wait_send)
        spread.rest(wait_send, False)


def sweep(transfer, respond, reflect, weighted, slabs):
    width, depth = transfer.shape
    rows = weighted.shape[0]
    peers = SIDE * SIDE
    share = rows // peers
    anywhere = pl.BlockSpec(memory_space=pl.ANY)
    vmem = pl.BlockSpec(memory_space=pltpu.VMEM)
    dma = pltpu.SemaphoreType.DMA
    operator = pltpu.VMEM((width, width), bf16)
    narrow = pltpu.VMEM((share, width), bf16)
    full = pltpu.VMEM((share, width), f32)
    return pl.pallas_call(
        functools.partial(sweep_kernel, slabs),
        out_shape=jax.ShapeDtypeStruct((rows, depth), bf16),
        in_specs=[anywhere] * 4,
        out_specs=vmem,
        scratch_shapes=[
            operator,
            operator,
            operator,
            pltpu.VMEM((width, depth), bf16),
            pltpu.VMEM((width, depth), bf16),
            pltpu.VMEM((rows, width), bf16),
            pltpu.VMEM((rows, depth), f32),
            full,
            full,
            full,
            narrow,
            narrow,
            narrow,
            narrow,
            pltpu.VMEM((rows, width), bf16),
            full,
            pltpu.VMEM((rows, depth), f32),
            dma((4,)),
            dma,
            dma,
            dma((CHUNKS,)),
            dma((CHUNKS,)),
            dma,
            dma,
            dma((2, peers)),
            dma((2, peers)),
            dma((2, peers, 2)),
            dma((2, peers, 2)),
        ]
        + [dma((peers, 2))] * 20,
        compiler_params=pltpu.CompilerParams(
            collective_id=0, has_side_effects=True, vmem_limit_bytes=60 * 2**20
        ),
        name="sweep",
    )(transfer, respond, reflect, weighted)


def shards(slabs, transmission, reflection, response, sources, placement):
    own_sources = sources[0]
    ticks, batch, depth = own_sources.shape
    rows = ticks * batch
    slab = lax.axis_index("slab")
    distance = jnp.abs(slab - placement).astype(f32)
    weighting = 1.0 / (1.0 + distance)
    weighted = (own_sources.astype(f32) * weighting[:, :, None]).astype(bf16)
    combined = sweep(
        transmission[0], response[0], reflection[0], weighted.reshape(rows, depth), slabs
    )
    return combined.reshape(1, ticks, batch, depth)


def solution(mesh):
    slabs = mesh.shape["slab"]
    torus = Mesh(mesh.devices.reshape(slabs, SIDE, SIDE), ("slab",) + TRACE)
    return jax.shard_map(
        functools.partial(shards, slabs),
        mesh=torus,
        in_specs=(
            P("slab", None, TRACE),
            P("slab", None, TRACE),
            P("slab", None, TRACE),
            P("slab", None, None, TRACE),
            P(),
        ),
        out_specs=P("slab", None, None, TRACE),
        check_vma=False,
    )
```

```python
import functools

import jax
import jax.numpy as jnp
from jax import lax
from jax.experimental import pallas as pl
from jax.experimental.pallas import tpu as pltpu
from jax.sharding import Mesh
from jax.sharding import PartitionSpec as P

TRACE = ("trace_0", "trace_1")
MESH = pl.DeviceIdType.MESH
SIDE = 4
CHUNKS = 4
FUSE_FROM = 4
LAG = 2
bf16 = jnp.bfloat16
f32 = jnp.float32


def dot(a, b):
    return jnp.dot(a, b, preferred_element_type=f32)


def loop(count, body):
    def step(i, carry):
        body(i)
        return carry

    lax.fori_loop(0, count, step, 0)


class Spread:
    def __init__(self, place, own, view, sems, extra=None):
        self.slab, self.row, self.col = place
        self.own, self.view, self.extra = own, view, extra
        self.arrived, self.up, self.down, self.fore, self.back = sems

    def copies(self, source, block, half, up, down, fore, back, run):
        row, col = self.row, self.col

        def send(sem, device):
            run(
                pltpu.make_async_remote_copy(
                    src_ref=source,
                    dst_ref=self.view(block, half),
                    send_sem=sem.at[block, half],
                    recv_sem=self.arrived.at[block, half],
                    device_id=device,
                    device_id_type=MESH,
                )
            )

        @pl.when(up)
        def _():
            send(self.up, (self.slab, row, jnp.minimum(col + 1, SIDE - 1)))

        @pl.when(down)
        def _():
            send(self.down, (self.slab, row, jnp.maximum(col - 1, 0)))

        @pl.when(fore)
        def _():
            send(self.fore, (self.slab, (row + 1) % SIDE, col))

        @pl.when(back)
        def _():
            send(self.back, (self.slab, (row + SIDE - 1) % SIDE, col))

        if self.extra is not None:
            run(self.extra(source, block, half))

    def await_piece(self, block, half):
        piece = self.view(block, half)
        pltpu.make_async_copy(piece, piece, self.arrived.at[block, half]).wait()

    def first(self, run):
        yes = self.row >= 0
        block = self.row * SIDE + self.col

        def piece(half):
            self.copies(self.own(half), block, half, self.col < SIDE - 1, self.col > 0, yes, yes, run)

        loop(2, piece)

    def handle(self, block, half, up, down, fore, back, run, receive):
        if receive:
            self.await_piece(block, half)
        self.copies(self.view(block, half), block, half, up, down, fore, back, run)

    def pieces(self, distance, body):
        def one(i):
            side = 2 * (i // 2) - 1
            at = self.col + side * distance
            there = (at >= 0) & (at < SIDE) & (distance >= 0) & ((distance > 0) | (side < 0))

            @pl.when(there)
            def _():
                body(side, at, i % 2)

        loop(4, one)

    def turn(self, r, run, receive):
        row, col = self.row, self.col
        no = row < 0

        def handed(at, half):
            inner = ((col == 1) & (at == 0)) | ((col == SIDE - 2) & (at == SIDE - 1))
            return inner & (half == 0)

        def lifted(at, half):
            mine = (at == col) & (half == 0)
            return mine & (col == 0), mine & (col == SIDE - 1)

        def along(side, at, half):
            up = (side < 0) & (col < SIDE - 1)
            down = (side > 0) & (col > 0)
            spread = jnp.logical_not(handed(at, half))
            self.handle(row * SIDE + at, half, up, down, spread, spread, run, receive)

        def around(side, at, half):
            up, down = lifted(at, half)
            fore = (half == 0) & jnp.logical_not(handed(at, half))
            self.handle((row + SIDE - 1) % SIDE * SIDE + at, half, up, down, fore, no, run, receive)
            self.handle((row + 1) % SIDE * SIDE + at, half, up, down, no, half == 1, run, receive)

        def across(side, at, half):
            up, down = lifted(at, half)
            self.handle((row + 2) % SIDE * SIDE + at, half, up, down, no, no, run, receive)

        @pl.when(r < SIDE - 1)
        def _():
            self.pieces(r + 1, along)

        self.pieces(r, around)
        self.pieces(r - 1, across)

    def rest(self, run, receive):
        loop(SIDE + 1, lambda r: self.turn(r, run, receive))


def start(copy):
    copy.start()


def wait_send(copy):
    copy.wait_send()


def sweep_kernel(
    slabs,
    transfer_ref,
    respond_ref,
    reflect_ref,
    weighted_ref,
    out_ref,
    t_own,
    t_oth,
    fused,
    respond,
    reflect,
    sources,
    driven,
    drv_own,
    drv_oth,
    local,
    x_in,
    z_out,
    z_in,
    y_own,
    contrast,
    total,
    totals,
    load_sem,
    d_send,
    d_recv,
    x_send,
    x_recv,
    z_send,
    z_recv,
    exchange_send,
    exchange_recv,
    core_send,
    core_recv,
    *spread_sems,
):
    slab = lax.axis_index("slab")
    row = lax.axis_index("trace_0")
    col = lax.axis_index("trace_1")
    trace = row * SIDE + col
    peers = SIDE * SIDE
    core = slab % 2
    chip = slab // 2
    last = slabs // 2 - 1
    place = chip * (1 - 2 * core) + last * core
    partner = (slab + 1 - 2 * core, row, col)
    following = ((slab + 2 - 4 * core + slabs) % slabs, row, col)
    previous = ((slab - 2 + 4 * core + slabs) % slabs, row, col)
    width = t_own.shape[0]
    depth = respond.shape[1]
    rows = sources.shape[0]
    share = rows // peers
    step = width // CHUNKS

    def peer(j):
        other = (trace + 1 + j) % peers
        return other, (slab, other // SIDE, other % SIDE)

    barrier = pltpu.get_barrier_semaphore()

    def greet(j):
        pl.semaphore_signal(barrier, inc=1, device_id=peer(j)[1], device_id_type=MESH)

    for device in (partner, following, previous):
        pl.semaphore_signal(barrier, inc=1, device_id=device, device_id_type=MESH)
    loop(peers - 1, greet)

    def block_columns(b):
        return pl.ds(pl.multiple_of(b * depth, depth), depth)

    def block_rows(b):
        return pl.ds(pl.multiple_of(b * share, share), share)

    loads = [
        pltpu.make_async_copy(transfer_ref, t_own.at[:, block_columns(trace)], load_sem.at[0]),
        pltpu.make_async_copy(weighted_ref, sources.at[:, block_columns(trace)], load_sem.at[1]),
        pltpu.make_async_copy(respond_ref, respond, load_sem.at[2]),
        pltpu.make_async_copy(reflect_ref, reflect, load_sem.at[3]),
    ]
    for load in loads:
        load.start()
    pl.semaphore_wait(barrier, peers + 2)

    def half_rows(count, half):
        return pl.ds(pl.multiple_of(half * (count // 2), count // 2), count // 2)

    here = (slab, row, col)

    def to_partner(source, block, half):
        return pltpu.make_async_remote_copy(
            src_ref=source,
            dst_ref=t_oth.at[half_rows(width, half), block_columns(block)],
            send_sem=core_send.at[block, half],
            recv_sem=core_recv.at[block, half],
            device_id=partner,
            device_id_type=MESH,
        )

    source_spread = Spread(
        here,
        lambda half: weighted_ref.at[half_rows(rows, half), :],
        lambda block, half: sources.at[half_rows(rows, half), block_columns(block)],
        spread_sems[0:5],
    )
    transfer_spread = Spread(
        here,
        lambda half: transfer_ref.at[half_rows(width, half), :],
        lambda block, half: t_own.at[half_rows(width, half), block_columns(block)],
        spread_sems[5:10],
        to_partner,
    )
    contrast_spread = Spread(
        here,
        lambda half: contrast.at[block_rows(trace), half_rows(width, half)],
        lambda block, half: contrast.at[block_rows(block), half_rows(width, half)],
        spread_sems[10:15],
    )

    def give_driven(j):
        other, device = peer(j)
        return pltpu.make_async_remote_copy(
            src_ref=driven.at[block_rows(other), :],
            dst_ref=drv_own.at[:, block_columns(trace)],
            send_sem=exchange_send.at[0, other],
            recv_sem=exchange_recv.at[0, trace],
            device_id=device,
            device_id_type=MESH,
        )

    def take_driven(j):
        other, _ = peer(j)
        piece = drv_own.at[:, block_columns(other)]
        pltpu.make_async_copy(piece, piece, exchange_recv.at[0, other]).wait()

    give_d = pltpu.make_async_remote_copy(
        src_ref=drv_own, dst_ref=drv_oth, send_sem=d_send, recv_sem=d_recv, device_id=partner, device_id_type=MESH
    )

    source_spread.first(start)
    transfer_spread.first(start)
    turns = SIDE + 1
    for load in loads:
        load.wait()

    def gather(i):
        @pl.when(i < turns)
        def _():
            source_spread.turn(i, start, True)

        @pl.when(i == turns)
        def _():
            driven[...] = dot(sources[...], respond[...])
            loop(peers - 1, lambda j: give_driven(j).start())
            drv_own[:, block_columns(trace)] = driven[block_rows(trace), :]

        @pl.when(i == turns + LAG - 1)
        def _():
            loop(peers - 1, take_driven)
            give_d.start()

        @pl.when(i >= LAG)
        def _():
            transfer_spread.turn(i - LAG, start, True)

    loop(turns + LAG, gather)

    def take_transfer(i):
        piece = t_oth.at[half_rows(width, i % 2), block_columns(i // 2)]
        pltpu.make_async_copy(piece, piece, core_recv.at[i // 2, i % 2]).wait()

    loop(2 * peers, take_transfer)
    give_d.wait()

    def columns(j):
        return pl.ds(j * step, step)

    def onward(j):
        return pltpu.make_async_remote_copy(
            src_ref=z_out.at[:, columns(j)],
            dst_ref=x_in.at[:, columns(j)],
            send_sem=x_send.at[j],
            recv_sem=x_recv.at[j],
            device_id=following,
            device_id_type=MESH,
        )

    def emit(j, value):
        z_out[:, columns(j)] = value.astype(bf16)

        @pl.when(place < last)
        def _():
            onward(j).start()

    @pl.when(place == 0)
    def _():
        y_own[...] = drv_own[...].astype(bf16)
        for j in range(CHUNKS):
            emit(j, dot(y_own[...], t_oth[:, columns(j)]) + drv_oth[:, columns(j)])

    def take_rows(operator, store):
        final = CHUNKS - 1
        for j in range(final):
            onward(j).wait_recv()
            local[...] += dot(x_in[:, columns(j)], operator[columns(j), :])
        onward(final).wait_recv()
        for j in range(CHUNKS):
            store(j, local[:, columns(j)] + dot(x_in[:, columns(final)], operator[columns(final), columns(j)]))

    def keep(j, value):
        y_own[:, columns(j)] = value.astype(bf16)

    @pl.when((place > 0) & (place < FUSE_FROM))
    def _():
        local[...] = drv_own[...]
        take_rows(t_own, keep)
        for j in range(CHUNKS):
            emit(j, dot(y_own[...], t_oth[:, columns(j)]) + drv_oth[:, columns(j)])

    @pl.when(place >= FUSE_FROM)
    def _():
        local[...] = dot(drv_own[...].astype(bf16), t_oth[...]) + drv_oth[...]
        wide = width // 8

        def block(i):
            to = pl.ds(pl.multiple_of(i * wide, wide), wide)
            fused[:, to] = dot(t_own[...], t_oth[:, to]).astype(bf16)

        loop(8, block)
        take_rows(fused, emit)
        for j in range(CHUNKS):
            keep(j, dot(x_in[...], t_own[:, columns(j)]) + drv_own[:, columns(j)])

    swap = pltpu.make_async_remote_copy(
        src_ref=z_out, dst_ref=z_in, send_sem=z_send, recv_sem=z_recv, device_id=partner, device_id_type=MESH
    )
    swap.start()
    swap.wait()
    mine = y_own[...].astype(f32)
    other_way = z_in[...].astype(f32)
    sign = (1 - 2 * core).astype(f32)
    contrast[block_rows(trace), :] = ((mine - other_way) * sign).astype(bf16)
    total[...] = mine + other_way
    contrast_spread.first(start)

    def give_total(j):
        other, device = peer(j)
        return pltpu.make_async_remote_copy(
            src_ref=total.at[:, block_columns(other)],
            dst_ref=totals.at[block_rows(trace), :],
            send_sem=exchange_send.at[1, other],
            recv_sem=exchange_recv.at[1, trace],
            device_id=device,
            device_id_type=MESH,
        )

    loop(peers - 1, lambda j: give_total(j).start())
    totals[block_rows(trace), :] = total[:, block_columns(trace)]
    contrast_spread.rest(start, True)

    def take_total(j):
        other, _ = peer(j)
        piece = totals.at[block_rows(other), :]
        pltpu.make_async_copy(piece, piece, exchange_recv.at[1, other]).wait()

    loop(peers - 1, take_total)
    out_ref[...] = (totals[...] + dot(contrast[...], reflect[...])).astype(bf16)

    @pl.when(place < last)
    def _():
        for j in range(CHUNKS):
            onward(j).wait_send()

    loop(peers - 1, lambda j: give_driven(j).wait_send())
    loop(peers - 1, lambda j: give_total(j).wait_send())
    for spread in (source_spread, transfer_spread, contrast_spread):
        spread.first(wait_send)
        spread.rest(wait_send, False)


def sweep(transfer, respond, reflect, weighted, slabs):
    width, depth = transfer.shape
    rows = weighted.shape[0]
    peers = SIDE * SIDE
    share = rows // peers
    anywhere = pl.BlockSpec(memory_space=pl.ANY)
    vmem = pl.BlockSpec(memory_space=pltpu.VMEM)
    dma = pltpu.SemaphoreType.DMA
    operator = pltpu.VMEM((width, width), bf16)
    narrow = pltpu.VMEM((share, width), bf16)
    full = pltpu.VMEM((share, width), f32)
    return pl.pallas_call(
        functools.partial(sweep_kernel, slabs),
        out_shape=jax.ShapeDtypeStruct((rows, depth), bf16),
        in_specs=[anywhere] * 4,
        out_specs=vmem,
        scratch_shapes=[
            operator,
            operator,
            operator,
            pltpu.VMEM((width, depth), bf16),
            pltpu.VMEM((width, depth), bf16),
            pltpu.VMEM((rows, width), bf16),
            pltpu.VMEM((rows, depth), f32),
            full,
            full,
            full,
            narrow,
            narrow,
            narrow,
            narrow,
            pltpu.VMEM((rows, width), bf16),
            full,
            pltpu.VMEM((rows, depth), f32),
            dma((4,)),
            dma,
            dma,
            dma((CHUNKS,)),
            dma((CHUNKS,)),
            dma,
            dma,
            dma((2, peers)),
            dma((2, peers)),
            dma((peers, 2)),
            dma((peers, 2)),
        ]
        + [dma((peers, 2))] * 15,
        compiler_params=pltpu.CompilerParams(
            collective_id=0, has_side_effects=True, vmem_limit_bytes=60 * 2**20
        ),
        name="sweep",
    )(transfer, respond, reflect, weighted)


def shards(slabs, transmission, reflection, response, sources, placement):
    own_sources = sources[0]
    ticks, batch, depth = own_sources.shape
    rows = ticks * batch
    slab = lax.axis_index("slab")
    distance = jnp.abs(slab - placement).astype(f32)
    weighting = 1.0 / (1.0 + distance)
    weighted = (own_sources.astype(f32) * weighting[:, :, None]).astype(bf16)
    combined = sweep(
        transmission[0], response[0], reflection[0], weighted.reshape(rows, depth), slabs
    )
    return combined.reshape(1, ticks, batch, depth)


def solution(mesh):
    slabs = mesh.shape["slab"]
    torus = Mesh(mesh.devices.reshape(slabs, SIDE, SIDE), ("slab",) + TRACE)
    return jax.shard_map(
        functools.partial(shards, slabs),
        mesh=torus,
        in_specs=(
            P("slab", None, TRACE),
            P("slab", None, TRACE),
            P("slab", None, TRACE),
            P("slab", None, None, TRACE),
            P(),
        ),
        out_specs=P("slab", None, None, TRACE),
        check_vma=False,
    )
```

```python
import functools

import jax
import jax.numpy as jnp
from jax import lax
from jax.experimental import pallas as pl
from jax.experimental.pallas import tpu as pltpu
from jax.sharding import Mesh
from jax.sharding import PartitionSpec as P

TRACE = ("trace_0", "trace_1")
MESH = pl.DeviceIdType.MESH
SIDE = 4
CHUNKS = 4
FUSE_FROM = 4
LAG = 2
bf16 = jnp.bfloat16
f32 = jnp.float32


def dot(a, b):
    return jnp.dot(a, b, preferred_element_type=f32)


def loop(count, body):
    def step(i, carry):
        body(i)
        return carry

    lax.fori_loop(0, count, step, 0)


class Spread:
    def __init__(self, place, own, view, sems, extra=None):
        self.slab, self.row, self.col = place
        self.own, self.view, self.extra = own, view, extra
        self.arrived, self.up, self.down, self.fore, self.back = sems

    def copies(self, source, block, half, up, down, fore, back, run):
        row, col = self.row, self.col

        def send(sem, device):
            run(
                pltpu.make_async_remote_copy(
                    src_ref=source,
                    dst_ref=self.view(block, half),
                    send_sem=sem.at[block, half],
                    recv_sem=self.arrived.at[block, half],
                    device_id=device,
                    device_id_type=MESH,
                )
            )

        @pl.when(up)
        def _():
            send(self.up, (self.slab, row, jnp.minimum(col + 1, SIDE - 1)))

        @pl.when(down)
        def _():
            send(self.down, (self.slab, row, jnp.maximum(col - 1, 0)))

        @pl.when(fore)
        def _():
            send(self.fore, (self.slab, (row + 1) % SIDE, col))

        @pl.when(back)
        def _():
            send(self.back, (self.slab, (row + SIDE - 1) % SIDE, col))

        if self.extra is not None and run is start:
            start(self.extra(source, block, half))

    def await_piece(self, block, half):
        piece = self.view(block, half)
        pltpu.make_async_copy(piece, piece, self.arrived.at[block, half]).wait()

    def first(self, run):
        yes = self.row >= 0
        block = self.row * SIDE + self.col

        def piece(half):
            self.copies(self.own(half), block, half, self.col < SIDE - 1, self.col > 0, yes, yes, run)

        loop(2, piece)

    def handle(self, block, half, up, down, fore, back, run, receive):
        if receive:
            self.await_piece(block, half)
        self.copies(self.view(block, half), block, half, up, down, fore, back, run)

    def pieces(self, distance, body):
        def one(i):
            side = 2 * (i // 2) - 1
            at = self.col + side * distance
            there = (at >= 0) & (at < SIDE) & (distance >= 0) & ((distance > 0) | (side < 0))

            @pl.when(there)
            def _():
                body(side, at, i % 2)

        loop(4, one)

    def turn(self, r, run, receive):
        row, col = self.row, self.col
        no = row < 0

        def handed(at, half):
            inner = ((col == 1) & (at == 0)) | ((col == SIDE - 2) & (at == SIDE - 1))
            return inner & (half == 0)

        def lifted(at, half):
            mine = (at == col) & (half == 0)
            return mine & (col == 0), mine & (col == SIDE - 1)

        def along(side, at, half):
            up = (side < 0) & (col < SIDE - 1)
            down = (side > 0) & (col > 0)
            spread = jnp.logical_not(handed(at, half))
            self.handle(row * SIDE + at, half, up, down, spread, spread, run, receive)

        def around(side, at, half):
            up, down = lifted(at, half)
            fore = (half == 0) & jnp.logical_not(handed(at, half))
            self.handle((row + SIDE - 1) % SIDE * SIDE + at, half, up, down, fore, no, run, receive)
            self.handle((row + 1) % SIDE * SIDE + at, half, up, down, no, half == 1, run, receive)

        def across(side, at, half):
            up, down = lifted(at, half)
            self.handle((row + 2) % SIDE * SIDE + at, half, up, down, no, no, run, receive)

        @pl.when(r < SIDE - 1)
        def _():
            self.pieces(r + 1, along)

        self.pieces(r, around)
        self.pieces(r - 1, across)

    def rest(self, run, receive):
        loop(SIDE + 1, lambda r: self.turn(r, run, receive))


def await_bytes(piece, sem):
    pltpu.make_async_copy(piece, piece, sem).wait()


def start(copy):
    copy.start()


def wait_send(copy):
    copy.wait_send()


def sweep_kernel(
    slabs,
    transfer_ref,
    respond_ref,
    reflect_ref,
    weighted_ref,
    out_ref,
    t_own,
    t_oth,
    fused,
    respond,
    reflect,
    sources,
    driven,
    drv_own,
    drv_oth,
    local,
    x_in,
    z_out,
    z_in,
    y_own,
    contrast,
    total,
    totals,
    load_sem,
    d_send,
    d_recv,
    x_send,
    x_recv,
    z_send,
    z_recv,
    exchange_send,
    exchange_recv,
    core_send,
    core_recv,
    *spread_sems,
):
    slab = lax.axis_index("slab")
    row = lax.axis_index("trace_0")
    col = lax.axis_index("trace_1")
    trace = row * SIDE + col
    peers = SIDE * SIDE
    core = slab % 2
    chip = slab // 2
    last = slabs // 2 - 1
    middle = max(slabs // 4, FUSE_FROM)
    place = chip * (1 - 2 * core) + last * core
    partner = (slab + 1 - 2 * core, row, col)
    following = ((slab + 2 - 4 * core + slabs) % slabs, row, col)
    previous = ((slab - 2 + 4 * core + slabs) % slabs, row, col)
    width = t_own.shape[0]
    depth = respond.shape[1]
    rows = sources.shape[0]
    share = rows // peers
    step = width // CHUNKS

    def peer(j):
        other = (trace + 1 + j) % peers
        return other, (slab, other // SIDE, other % SIDE)

    barrier = pltpu.get_barrier_semaphore()

    def greet(j):
        pl.semaphore_signal(barrier, inc=1, device_id=peer(j)[1], device_id_type=MESH)

    for device in (partner, following, previous):
        pl.semaphore_signal(barrier, inc=1, device_id=device, device_id_type=MESH)
    loop(peers - 1, greet)

    def block_columns(b):
        return pl.ds(pl.multiple_of(b * depth, depth), depth)

    def block_rows(b):
        return pl.ds(pl.multiple_of(b * share, share), share)

    loads = [
        pltpu.make_async_copy(transfer_ref, t_own.at[:, block_columns(trace)], load_sem.at[0]),
        pltpu.make_async_copy(weighted_ref, sources.at[:, block_columns(trace)], load_sem.at[1]),
        pltpu.make_async_copy(respond_ref, respond, load_sem.at[2]),
        pltpu.make_async_copy(reflect_ref, reflect, load_sem.at[3]),
    ]
    for load in loads:
        load.start()
    pl.semaphore_wait(barrier, peers + 2)

    def half_rows(count, half):
        return pl.ds(pl.multiple_of(half * (count // 2), count // 2), count // 2)

    here = (slab, row, col)

    def to_partner(source, block, half):
        return pltpu.make_async_remote_copy(
            src_ref=source,
            dst_ref=t_oth.at[half_rows(width, half), block_columns(block)],
            send_sem=core_send,
            recv_sem=core_recv,
            device_id=partner,
            device_id_type=MESH,
        )

    source_spread = Spread(
        here,
        lambda half: weighted_ref.at[half_rows(rows, half), :],
        lambda block, half: sources.at[half_rows(rows, half), block_columns(block)],
        spread_sems[0:5],
    )
    transfer_spread = Spread(
        here,
        lambda half: transfer_ref.at[half_rows(width, half), :],
        lambda block, half: t_own.at[half_rows(width, half), block_columns(block)],
        spread_sems[5:10],
        to_partner,
    )
    contrast_spread = Spread(
        here,
        lambda half: contrast.at[block_rows(trace), half_rows(width, half)],
        lambda block, half: contrast.at[block_rows(block), half_rows(width, half)],
        spread_sems[10:15],
    )

    def give_driven(j):
        other, device = peer(j)
        return pltpu.make_async_remote_copy(
            src_ref=driven.at[block_rows(other), :],
            dst_ref=drv_own.at[:, block_columns(trace)],
            send_sem=exchange_send.at[0],
            recv_sem=exchange_recv.at[0],
            device_id=device,
            device_id_type=MESH,
        )

    give_d = pltpu.make_async_remote_copy(
        src_ref=drv_own, dst_ref=drv_oth, send_sem=d_send, recv_sem=d_recv, device_id=partner, device_id_type=MESH
    )

    source_spread.first(start)
    transfer_spread.first(start)
    turns = SIDE + 1
    for load in loads:
        load.wait()

    def gather(i):
        @pl.when(i < turns)
        def _():
            source_spread.turn(i, start, True)

        @pl.when(i == turns)
        def _():
            driven[...] = dot(sources[...], respond[...])
            loop(peers - 1, lambda j: give_driven(j).start())
            drv_own[:, block_columns(trace)] = driven[block_rows(trace), :]

        @pl.when(i == turns + LAG - 1)
        def _():
            await_bytes(drv_own.at[:, pl.ds(0, (peers - 1) * depth)], exchange_recv.at[0])
            give_d.start()

        @pl.when(i >= LAG)
        def _():
            transfer_spread.turn(i - LAG, start, True)

    loop(turns + LAG, gather)

    await_bytes(t_oth, core_recv)
    give_d.wait()

    def columns(j):
        return pl.ds(j * step, step)

    def onward(j):
        return pltpu.make_async_remote_copy(
            src_ref=z_out.at[:, columns(j)],
            dst_ref=x_in.at[:, columns(j)],
            send_sem=x_send.at[j],
            recv_sem=x_recv.at[j],
            device_id=following,
            device_id_type=MESH,
        )

    def emit(j, value):
        z_out[:, columns(j)] = value.astype(bf16)

        @pl.when(place < last)
        def _():
            onward(j).start()

    swap = pltpu.make_async_remote_copy(
        src_ref=z_out, dst_ref=z_in, send_sem=z_send, recv_sem=z_recv, device_id=partner, device_id_type=MESH
    )

    def settle():
        for spread in (source_spread, transfer_spread):
            spread.first(wait_send)
            spread.rest(wait_send, False)
        await_bytes(t_own, core_send)
        await_bytes(driven.at[pl.ds(0, (peers - 1) * share), :], exchange_send.at[0])

    def take_rows(operator, store):
        final = CHUNKS - 1
        for j in range(final):
            onward(j).wait_recv()
            local[...] += dot(x_in[:, columns(j)], operator[columns(j), :])
        onward(final).wait_recv()
        for j in range(CHUNKS):
            store(j, local[:, columns(j)] + dot(x_in[:, columns(final)], operator[columns(final), columns(j)]))

    @pl.when(place == 0)
    def _():
        y_own[...] = drv_own[...].astype(bf16)
        for j in range(CHUNKS):
            emit(j, dot(y_own[...], t_oth[:, columns(j)]) + drv_oth[:, columns(j)])
        swap.start()

    def keep(j, value):
        y_own[:, columns(j)] = value.astype(bf16)

    @pl.when((place > 0) & (place < FUSE_FROM))
    def _():
        local[...] = drv_own[...]
        take_rows(t_own, keep)
        for j in range(CHUNKS):
            emit(j, dot(y_own[...], t_oth[:, columns(j)]) + drv_oth[:, columns(j)])
        swap.start()

    @pl.when(place >= FUSE_FROM)
    def _():
        local[...] = dot(drv_own[...].astype(bf16), t_oth[...]) + drv_oth[...]
        wide = width // 8

        def block(i):
            to = pl.ds(pl.multiple_of(i * wide, wide), wide)
            fused[:, to] = dot(t_own[...], t_oth[:, to]).astype(bf16)

        loop(8, block)

        @pl.when(place >= middle)
        def _():
            settle()

        take_rows(fused, emit)
        swap.start()
        for j in range(CHUNKS):
            keep(j, dot(x_in[...], t_own[:, columns(j)]) + drv_own[:, columns(j)])

    @pl.when(place < middle)
    def _():
        settle()

    swap.wait()
    mine = y_own[...].astype(f32)
    other_way = z_in[...].astype(f32)
    sign = (1 - 2 * core).astype(f32)
    contrast[block_rows(trace), :] = ((mine - other_way) * sign).astype(bf16)
    total[...] = mine + other_way
    contrast_spread.first(start)

    def give_total(j):
        other, device = peer(j)
        return pltpu.make_async_remote_copy(
            src_ref=total.at[:, block_columns(other)],
            dst_ref=totals.at[block_rows(trace), :],
            send_sem=exchange_send.at[1],
            recv_sem=exchange_recv.at[1],
            device_id=device,
            device_id_type=MESH,
        )

    loop(peers - 1, lambda j: give_total(j).start())
    totals[block_rows(trace), :] = total[:, block_columns(trace)]
    contrast_spread.rest(start, True)

    await_bytes(totals.at[pl.ds(0, (peers - 1) * share), :], exchange_recv.at[1])
    out_ref[...] = (totals[...] + dot(contrast[...], reflect[...])).astype(bf16)

    @pl.when(place < last)
    def _():
        for j in range(CHUNKS):
            onward(j).wait_send()

    await_bytes(total.at[:, pl.ds(0, (peers - 1) * depth)], exchange_send.at[1])
    contrast_spread.first(wait_send)
    contrast_spread.rest(wait_send, False)


def sweep(transfer, respond, reflect, weighted, slabs):
    width, depth = transfer.shape
    rows = weighted.shape[0]
    peers = SIDE * SIDE
    share = rows // peers
    anywhere = pl.BlockSpec(memory_space=pl.ANY)
    hbm = pl.BlockSpec(memory_space=pltpu.HBM)
    vmem = pl.BlockSpec(memory_space=pltpu.VMEM)
    dma = pltpu.SemaphoreType.DMA
    operator = pltpu.VMEM((width, width), bf16)
    narrow = pltpu.VMEM((share, width), bf16)
    full = pltpu.VMEM((share, width), f32)
    return pl.pallas_call(
        functools.partial(sweep_kernel, slabs),
        out_shape=jax.ShapeDtypeStruct((rows, depth), bf16),
        in_specs=[hbm, hbm, hbm, anywhere],
        out_specs=vmem,
        scratch_shapes=[
            operator,
            operator,
            operator,
            pltpu.VMEM((width, depth), bf16),
            pltpu.VMEM((width, depth), bf16),
            pltpu.VMEM((rows, width), bf16),
            pltpu.VMEM((rows, depth), f32),
            full,
            full,
            full,
            narrow,
            narrow,
            narrow,
            narrow,
            pltpu.VMEM((rows, width), bf16),
            full,
            pltpu.VMEM((rows, depth), f32),
            dma((4,)),
            dma,
            dma,
            dma((CHUNKS,)),
            dma((CHUNKS,)),
            dma,
            dma,
            dma((2,)),
            dma((2,)),
            dma,
            dma,
        ]
        + [dma((peers, 2))] * 15,
        compiler_params=pltpu.CompilerParams(
            collective_id=0, has_side_effects=True, vmem_limit_bytes=60 * 2**20
        ),
        name="sweep",
    )(transfer, respond, reflect, weighted)


def shards(slabs, transmission, reflection, response, sources, placement):
    own_sources = sources[0]
    ticks, batch, depth = own_sources.shape
    rows = ticks * batch
    slab = lax.axis_index("slab")
    distance = jnp.abs(slab - placement).astype(f32)
    weighting = 1.0 / (1.0 + distance)
    weighted = (own_sources.astype(f32) * weighting[:, :, None]).astype(bf16)
    combined = sweep(
        transmission[0], response[0], reflection[0], weighted.reshape(rows, depth), slabs
    )
    return combined.reshape(1, ticks, batch, depth)


def solution(mesh):
    slabs = mesh.shape["slab"]
    torus = Mesh(mesh.devices.reshape(slabs, SIDE, SIDE), ("slab",) + TRACE)
    return jax.shard_map(
        functools.partial(shards, slabs),
        mesh=torus,
        in_specs=(
            P("slab", None, TRACE),
            P("slab", None, TRACE),
            P("slab", None, TRACE),
            P("slab", None, None, TRACE),
            P(),
        ),
        out_specs=P("slab", None, None, TRACE),
        check_vma=False,
    )
```

```python
import functools

import jax
import jax.numpy as jnp
from jax import lax
from jax.experimental import pallas as pl
from jax.experimental.pallas import tpu as pltpu
from jax.sharding import Mesh
from jax.sharding import PartitionSpec as P

TRACE = ("trace_0", "trace_1")
MESH = pl.DeviceIdType.MESH
SIDE = 4
CHUNKS = 4
FUSE_FROM = 4
LAG = 2
bf16 = jnp.bfloat16
f32 = jnp.float32


def dot(a, b):
    return jnp.dot(a, b, preferred_element_type=f32)


def loop(count, body):
    def step(i, carry):
        body(i)
        return carry

    lax.fori_loop(0, count, step, 0)


class Spread:
    def __init__(self, place, own, view, sems, extra=None):
        self.slab, self.row, self.col = place
        self.own, self.view, self.extra = own, view, extra
        self.arrived, self.up, self.down, self.fore, self.back = sems

    def copies(self, source, block, half, up, down, fore, back, run):
        row, col = self.row, self.col

        def send(sem, device):
            run(
                pltpu.make_async_remote_copy(
                    src_ref=source,
                    dst_ref=self.view(block, half),
                    send_sem=sem.at[block, half],
                    recv_sem=self.arrived.at[block, half],
                    device_id=device,
                    device_id_type=MESH,
                )
            )

        @pl.when(up)
        def _():
            send(self.up, (self.slab, row, jnp.minimum(col + 1, SIDE - 1)))

        @pl.when(down)
        def _():
            send(self.down, (self.slab, row, jnp.maximum(col - 1, 0)))

        @pl.when(fore)
        def _():
            send(self.fore, (self.slab, (row + 1) % SIDE, col))

        @pl.when(back)
        def _():
            send(self.back, (self.slab, (row + SIDE - 1) % SIDE, col))

        if self.extra is not None and run is start:
            start(self.extra(source, block, half))

    def await_piece(self, block, half):
        piece = self.view(block, half)
        pltpu.make_async_copy(piece, piece, self.arrived.at[block, half]).wait()

    def first(self, run):
        yes = self.row >= 0
        block = self.row * SIDE + self.col

        def piece(half):
            self.copies(self.own(half), block, half, self.col < SIDE - 1, self.col > 0, yes, yes, run)

        loop(2, piece)

    def handle(self, block, half, up, down, fore, back, run, receive):
        if receive:
            self.await_piece(block, half)
        self.copies(self.view(block, half), block, half, up, down, fore, back, run)

    def pieces(self, distance, body):
        def one(i):
            side = 2 * (i // 2) - 1
            at = self.col + side * distance
            there = (at >= 0) & (at < SIDE) & (distance >= 0) & ((distance > 0) | (side < 0))

            @pl.when(there)
            def _():
                body(side, at, i % 2)

        loop(4, one)

    def turn(self, r, run, receive):
        row, col = self.row, self.col
        no = row < 0

        def handed(at, half):
            inner = ((col == 1) & (at == 0)) | ((col == SIDE - 2) & (at == SIDE - 1))
            return inner & (half == 0)

        def lifted(at, half):
            mine = (at == col) & (half == 0)
            return mine & (col == 0), mine & (col == SIDE - 1)

        def along(side, at, half):
            up = (side < 0) & (col < SIDE - 1)
            down = (side > 0) & (col > 0)
            spread = jnp.logical_not(handed(at, half))
            self.handle(row * SIDE + at, half, up, down, spread, spread, run, receive)

        def around(side, at, half):
            up, down = lifted(at, half)
            fore = (half == 0) & jnp.logical_not(handed(at, half))
            self.handle((row + SIDE - 1) % SIDE * SIDE + at, half, up, down, fore, no, run, receive)
            self.handle((row + 1) % SIDE * SIDE + at, half, up, down, no, half == 1, run, receive)

        def across(side, at, half):
            up, down = lifted(at, half)
            self.handle((row + 2) % SIDE * SIDE + at, half, up, down, no, no, run, receive)

        @pl.when(r < SIDE - 1)
        def _():
            self.pieces(r + 1, along)

        self.pieces(r, around)
        self.pieces(r - 1, across)

    def rest(self, run, receive):
        loop(SIDE + 1, lambda r: self.turn(r, run, receive))


def await_bytes(piece, sem):
    pltpu.make_async_copy(piece, piece, sem).wait()


def start(copy):
    copy.start()


def wait_send(copy):
    copy.wait_send()


def sweep_kernel(
    slabs,
    transfer_ref,
    respond_ref,
    reflect_ref,
    weighted_ref,
    out_ref,
    t_own,
    t_oth,
    fused,
    respond,
    reflect,
    sources,
    driven,
    drv_own,
    drv_oth,
    local,
    x_in,
    z_out,
    z_in,
    y_own,
    contrast,
    total,
    totals,
    load_sem,
    d_send,
    d_recv,
    x_send,
    x_recv,
    z_send,
    z_recv,
    exchange_send,
    exchange_recv,
    core_send,
    core_recv,
    *spread_sems,
):
    slab = lax.axis_index("slab")
    row = lax.axis_index("trace_0")
    col = lax.axis_index("trace_1")
    trace = row * SIDE + col
    peers = SIDE * SIDE
    core = slab % 2
    chip = slab // 2
    last = slabs // 2 - 1
    middle = max(slabs // 4, FUSE_FROM)
    place = chip * (1 - 2 * core) + last * core
    partner = (slab + 1 - 2 * core, row, col)
    following = ((slab + 2 - 4 * core + slabs) % slabs, row, col)
    previous = ((slab - 2 + 4 * core + slabs) % slabs, row, col)
    width = t_own.shape[0]
    depth = respond.shape[1]
    rows = sources.shape[0]
    share = rows // peers
    step = width // CHUNKS

    def peer(j):
        other = (trace + 1 + j) % peers
        return other, (slab, other // SIDE, other % SIDE)

    barrier = pltpu.get_barrier_semaphore()

    def greet(j):
        pl.semaphore_signal(barrier, inc=1, device_id=peer(j)[1], device_id_type=MESH)

    for device in (partner, following, previous):
        pl.semaphore_signal(barrier, inc=1, device_id=device, device_id_type=MESH)
    loop(peers - 1, greet)

    def block_columns(b):
        return pl.ds(pl.multiple_of(b * depth, depth), depth)

    def block_rows(b):
        return pl.ds(pl.multiple_of(b * share, share), share)

    loads = [
        pltpu.make_async_copy(transfer_ref, t_own.at[:, block_columns(trace)], load_sem.at[0]),
        pltpu.make_async_copy(weighted_ref, sources.at[:, block_columns(trace)], load_sem.at[1]),
        pltpu.make_async_copy(respond_ref, respond, load_sem.at[2]),
        pltpu.make_async_copy(reflect_ref, reflect, load_sem.at[3]),
    ]
    for load in loads:
        load.start()
    pl.semaphore_wait(barrier, peers + 2)

    def half_rows(count, half):
        return pl.ds(pl.multiple_of(half * (count // 2), count // 2), count // 2)

    here = (slab, row, col)

    def to_partner(source, block, half):
        return pltpu.make_async_remote_copy(
            src_ref=source,
            dst_ref=t_oth.at[half_rows(width, half), block_columns(block)],
            send_sem=core_send,
            recv_sem=core_recv,
            device_id=partner,
            device_id_type=MESH,
        )

    source_spread = Spread(
        here,
        lambda half: weighted_ref.at[half_rows(rows, half), :],
        lambda block, half: sources.at[half_rows(rows, half), block_columns(block)],
        spread_sems[0:5],
    )
    transfer_spread = Spread(
        here,
        lambda half: transfer_ref.at[half_rows(width, half), :],
        lambda block, half: t_own.at[half_rows(width, half), block_columns(block)],
        spread_sems[5:10],
        to_partner,
    )
    contrast_spread = Spread(
        here,
        lambda half: contrast.at[block_rows(trace), half_rows(width, half)],
        lambda block, half: contrast.at[block_rows(block), half_rows(width, half)],
        spread_sems[10:15],
    )

    def give_driven(j):
        other, device = peer(j)
        return pltpu.make_async_remote_copy(
            src_ref=driven.at[block_rows(other), :],
            dst_ref=drv_own.at[:, block_columns(trace)],
            send_sem=exchange_send.at[0],
            recv_sem=exchange_recv.at[0],
            device_id=device,
            device_id_type=MESH,
        )

    give_d = pltpu.make_async_remote_copy(
        src_ref=drv_own, dst_ref=drv_oth, send_sem=d_send, recv_sem=d_recv, device_id=partner, device_id_type=MESH
    )

    source_spread.first(start)
    transfer_spread.first(start)
    turns = SIDE + 1
    for load in loads:
        load.wait()

    def gather(i):
        @pl.when(i < turns)
        def _():
            source_spread.turn(i, start, True)

        @pl.when(i == turns)
        def _():
            driven[...] = dot(sources[...], respond[...])
            loop(peers - 1, lambda j: give_driven(j).start())
            drv_own[:, block_columns(trace)] = driven[block_rows(trace), :]

        @pl.when(i == turns + LAG - 1)
        def _():
            await_bytes(drv_own.at[:, pl.ds(0, (peers - 1) * depth)], exchange_recv.at[0])
            give_d.start()

        @pl.when(i >= LAG)
        def _():
            transfer_spread.turn(i - LAG, start, True)

    loop(turns + LAG, gather)

    await_bytes(t_oth, core_recv)
    give_d.wait()

    def columns(j):
        return pl.ds(j * step, step)

    def onward(j):
        return pltpu.make_async_remote_copy(
            src_ref=z_out.at[:, columns(j)],
            dst_ref=x_in.at[:, columns(j)],
            send_sem=x_send.at[j],
            recv_sem=x_recv.at[j],
            device_id=following,
            device_id_type=MESH,
        )

    def emit(j, value):
        z_out[:, columns(j)] = value.astype(bf16)

        @pl.when(place < last)
        def _():
            onward(j).start()

    swap = pltpu.make_async_remote_copy(
        src_ref=z_out, dst_ref=z_in, send_sem=z_send, recv_sem=z_recv, device_id=partner, device_id_type=MESH
    )

    def settle():
        for spread in (source_spread, transfer_spread):
            spread.first(wait_send)
            spread.rest(wait_send, False)
        await_bytes(t_own, core_send)
        await_bytes(driven.at[pl.ds(0, (peers - 1) * share), :], exchange_send.at[0])

    def take_rows(operator, store):
        final = CHUNKS - 1
        for j in range(final):
            onward(j).wait_recv()
            local[...] += dot(x_in[:, columns(j)], operator[columns(j), :])
        onward(final).wait_recv()
        for j in range(CHUNKS):
            store(j, local[:, columns(j)] + dot(x_in[:, columns(final)], operator[columns(final), columns(j)]))

    @pl.when(place == 0)
    def _():
        y_own[...] = drv_own[...].astype(bf16)
        for j in range(CHUNKS):
            emit(j, dot(y_own[...], t_oth[:, columns(j)]) + drv_oth[:, columns(j)])
        swap.start()

    def keep(j, value):
        y_own[:, columns(j)] = value.astype(bf16)

    @pl.when((place > 0) & (place < FUSE_FROM))
    def _():
        local[...] = drv_own[...]
        take_rows(t_own, keep)
        for j in range(CHUNKS):
            emit(j, dot(y_own[...], t_oth[:, columns(j)]) + drv_oth[:, columns(j)])
        swap.start()

    @pl.when(place >= FUSE_FROM)
    def _():
        local[...] = dot(drv_own[...].astype(bf16), t_oth[...]) + drv_oth[...]
        wide = width // 8

        def block(i):
            to = pl.ds(pl.multiple_of(i * wide, wide), wide)
            fused[:, to] = dot(t_own[...], t_oth[:, to]).astype(bf16)

        loop(8, block)

        @pl.when(place >= middle)
        def _():
            settle()

        take_rows(fused, emit)
        swap.start()
        for j in range(CHUNKS):
            keep(j, dot(x_in[...], t_own[:, columns(j)]) + drv_own[:, columns(j)])

    @pl.when(place < middle)
    def _():
        settle()

    swap.wait()
    mine = y_own[...].astype(f32)
    other_way = z_in[...].astype(f32)
    sign = (1 - 2 * core).astype(f32)
    contrast[block_rows(trace), :] = ((mine - other_way) * sign).astype(bf16)
    total[...] = mine + other_way
    contrast_spread.first(start)

    def give_total(j):
        other, device = peer(j)
        return pltpu.make_async_remote_copy(
            src_ref=total.at[:, block_columns(other)],
            dst_ref=totals.at[block_rows(trace), :],
            send_sem=exchange_send.at[1],
            recv_sem=exchange_recv.at[1],
            device_id=device,
            device_id_type=MESH,
        )

    totals[block_rows(trace), :] = total[:, block_columns(trace)]

    def finish(r):
        contrast_spread.turn(r, start, True)

        @pl.when(r == 0)
        def _():
            loop(peers - 1, lambda j: give_total(j).start())

        @pl.when(r >= 2)
        def _():
            contrast_spread.turn(r - 2, wait_send, False)

    loop(SIDE + 1, finish)

    await_bytes(totals.at[pl.ds(0, (peers - 1) * share), :], exchange_recv.at[1])
    out_ref[...] = (totals[...] + dot(contrast[...], reflect[...])).astype(bf16)

    @pl.when(place < last)
    def _():
        for j in range(CHUNKS):
            onward(j).wait_send()

    await_bytes(total.at[:, pl.ds(0, (peers - 1) * depth)], exchange_send.at[1])
    contrast_spread.first(wait_send)
    loop(2, lambda i: contrast_spread.turn(SIDE - 1 + i, wait_send, False))


def sweep(transfer, respond, reflect, weighted, slabs):
    width, depth = transfer.shape
    rows = weighted.shape[0]
    peers = SIDE * SIDE
    share = rows // peers
    anywhere = pl.BlockSpec(memory_space=pl.ANY)
    hbm = pl.BlockSpec(memory_space=pltpu.HBM)
    vmem = pl.BlockSpec(memory_space=pltpu.VMEM)
    dma = pltpu.SemaphoreType.DMA
    operator = pltpu.VMEM((width, width), bf16)
    narrow = pltpu.VMEM((share, width), bf16)
    full = pltpu.VMEM((share, width), f32)
    return pl.pallas_call(
        functools.partial(sweep_kernel, slabs),
        out_shape=jax.ShapeDtypeStruct((rows, depth), bf16),
        in_specs=[hbm, hbm, hbm, anywhere],
        out_specs=vmem,
        scratch_shapes=[
            operator,
            operator,
            operator,
            pltpu.VMEM((width, depth), bf16),
            pltpu.VMEM((width, depth), bf16),
            pltpu.VMEM((rows, width), bf16),
            pltpu.VMEM((rows, depth), f32),
            full,
            full,
            full,
            narrow,
            narrow,
            narrow,
            narrow,
            pltpu.VMEM((rows, width), bf16),
            full,
            pltpu.VMEM((rows, depth), f32),
            dma((4,)),
            dma,
            dma,
            dma((CHUNKS,)),
            dma((CHUNKS,)),
            dma,
            dma,
            dma((2,)),
            dma((2,)),
            dma,
            dma,
        ]
        + [dma((peers, 2))] * 15,
        compiler_params=pltpu.CompilerParams(
            collective_id=0, has_side_effects=True, vmem_limit_bytes=60 * 2**20
        ),
        name="sweep",
    )(transfer, respond, reflect, weighted)


def shards(slabs, transmission, reflection, response, sources, placement):
    own_sources = sources[0]
    ticks, batch, depth = own_sources.shape
    rows = ticks * batch
    slab = lax.axis_index("slab")
    distance = jnp.abs(slab - placement).astype(f32)
    weighting = 1.0 / (1.0 + distance)
    weighted = (own_sources.astype(f32) * weighting[:, :, None]).astype(bf16)
    combined = sweep(
        transmission[0], response[0], reflection[0], weighted.reshape(rows, depth), slabs
    )
    return combined.reshape(1, ticks, batch, depth)


def solution(mesh):
    slabs = mesh.shape["slab"]
    torus = Mesh(mesh.devices.reshape(slabs, SIDE, SIDE), ("slab",) + TRACE)
    return jax.shard_map(
        functools.partial(shards, slabs),
        mesh=torus,
        in_specs=(
            P("slab", None, TRACE),
            P("slab", None, TRACE),
            P("slab", None, TRACE),
            P("slab", None, None, TRACE),
            P(),
        ),
        out_specs=P("slab", None, None, TRACE),
        check_vma=False,
    )
```
